256 devices in a mesh: clip: 16 (over y, z_lo, core), text: 16 (over x, z_hi).
Axes of the slice: x: 4, y: 4, z: 8 (z_hi: 4, z_lo: 2; z = z_hi * 2 + z_lo), core: 2. Of those that a mesh axis runs over, the one named last changes fastest.
Arguments:
- clip_emb: bfloat16 [16384, 1152], P(('clip', 'text')), may hold values from -0.19921875 to 0.19921875
- text_emb: bfloat16 [16, 1024, 1152], P('text', 'clip'), may hold values from -0.19921875 to 0.19921875
- positive: int32 [16384], P('clip'), may hold values from 0 to 16383, each once
- log_temp: float32 [], replicated, may hold values from 2.3 to 3
- bias: float32 [], replicated, may hold values from -7 to -5
Outputs:
- loss: float32 [], replicated
- grad_clip: float32 [16384, 1152], P(('clip', 'text'))
- grad_text: float32 [16, 1024, 1152], P('text', 'clip')
- grad_temp: float32 [], replicated
- grad_bias: float32 [], replicated
The draws below stay inside these ranges and needn't reach their ends.
All inputs are finite; a program needn't handle non-finite values.
Results may differ from the reference program's by a relative error of at most 0.0044.
Values may be sent and summed in bfloat16 or wider, within the bound.
A program may use at most 64 MiB of HBM per device.

```python
import jax
import jax.numpy as jnp
from jax import lax

D = 1152
PAIRS = 16384
CLIP_ROWS = 1024
TEXT_ROWS = 1024
N_TEXT = 16


def steps_of(stream_key, extent, pieces, least, top_value):
    loudness, own = 1.0, jax.random.fold_in(stream_key, 6)
    for axis_at, blocks in pieces:
        heights = jnp.exp(jax.random.uniform(jax.random.fold_in(own, axis_at), (blocks,), jnp.float32, least / len(pieces), top_value / len(pieces)))
        loudness = loudness * jnp.repeat(heights, extent[axis_at] // blocks).reshape([-1 if axis == axis_at else 1 for axis in range(len(extent))])
    return loudness


def noise(stream_key, dims, width, reach, cuts=(), kind=jnp.bfloat16):
    array = jax.random.normal(stream_key, dims, jnp.float32) * width
    if len(cuts) > 0:
        array = steps_of(stream_key, dims, cuts, -0.22, 0.18) * array
    return jnp.clip(array, min=-reach, max=reach).astype(kind)


def setup_inputs(seed: int = 0) -> dict:
    seeds = jax.random.split(jax.random.key(seed), 6)
    clip_emb = noise(seeds[0], (PAIRS, D), 0.03, 0.19921875, ((0, 256),))
    text_emb = noise(seeds[1], (N_TEXT, TEXT_ROWS, D), 0.03, 0.19921875, ((0, 16), (1, 16)))
    positive = jax.random.permutation(seeds[2], PAIRS).astype(jnp.int32)
    log_temp = jnp.clip(jax.random.uniform(seeds[3], (), jnp.float32, 2.3, 3.0), 2.3, 3.0)
    bias = jnp.clip(jax.random.uniform(seeds[4], (), jnp.float32, -7.0, -5.0), -7.0, -5.0)
    return dict(clip_emb=clip_emb, text_emb=text_emb, positive=positive, log_temp=log_temp, bias=bias)


def unit_rows(emb):
    wide = emb.astype(jnp.float32)
    scale = lax.rsqrt(lax.optimization_barrier(jnp.sum(wide * wide, axis=1, keepdims=True)) + 1e-06)
    normal = wide * scale
    return (scale, normal, normal.astype(jnp.bfloat16))

def back_rows(scale, normal, upstream):
    return scale * (upstream - normal * lax.optimization_barrier(jnp.sum(normal * upstream, axis=1, keepdims=True)))

def reference(clip_emb, text_emb, positive, log_temp, bias):
    text_flat = text_emb.reshape(PAIRS, D)
    clip_scale, clip_norm, clip_unit = unit_rows(clip_emb)
    text_scale, text_norm, text_unit = unit_rows(text_flat)
    temp = jnp.exp(log_temp)
    blocks = PAIRS // CLIP_ROWS
    columns = jnp.arange(PAIRS, dtype=jnp.int32)

    def advance(carry, index):
        text_acc, loss_acc, bias_acc, temp_acc = carry
        begin = (index * CLIP_ROWS).astype(jnp.int32)
        rows = lax.dynamic_slice_in_dim(clip_unit, begin, CLIP_ROWS, 0)
        paired = lax.dynamic_slice_in_dim(positive, begin, CLIP_ROWS, 0)
        sims = lax.dot_general(rows, text_unit, (((1,), (1,)), ((), ())), preferred_element_type=jnp.float32)
        logits = temp * sims + bias
        sign = jnp.where(paired[:, None] == columns[None, :], 1.0, -1.0).astype(jnp.float32)
        loss_acc = loss_acc - jnp.sum(jax.nn.log_sigmoid(sign * logits))
        dlogit = -sign * jax.nn.sigmoid(-sign * logits)
        bias_acc = bias_acc + jnp.sum(dlogit)
        temp_acc = temp_acc + jnp.sum(dlogit * sims)
        dlogit_low = dlogit.astype(jnp.bfloat16)
        clip_part = jnp.dot(dlogit_low, text_unit, preferred_element_type=jnp.float32)
        text_acc = text_acc + lax.dot_general(dlogit_low, rows, (((0,), (0,)), ((), ())), preferred_element_type=jnp.float32)
        return ((text_acc, loss_acc, bias_acc, temp_acc), clip_part)
    start = (jnp.zeros((PAIRS, D), jnp.float32), jnp.float32(0.0), jnp.float32(0.0), jnp.float32(0.0))
    final, parts = lax.scan(advance, start, jnp.arange(blocks, dtype=jnp.int32))
    text_acc, loss_acc, bias_acc, temp_acc = final
    clip_back = temp * parts.reshape(PAIRS, D)
    text_back = temp * text_acc
    grad_clip = back_rows(clip_scale, clip_norm, clip_back)
    grad_text = back_rows(text_scale, text_norm, text_back).reshape(N_TEXT, TEXT_ROWS, D)
    loss = loss_acc / PAIRS
    grad_temp = temp * temp_acc / PAIRS
    grad_bias = bias_acc / PAIRS
    return (loss, grad_clip, grad_text, grad_temp, grad_bias)
```

```python
import jax
import jax.numpy as jnp
from jax import lax
from jax.experimental import pallas as pl
from jax.experimental.pallas import tpu as pltpu
from jax.sharding import PartitionSpec as P

MESH = pl.DeviceIdType.MESH
F32 = jnp.float32
BF16 = jnp.bfloat16
LOG2E = 1.4426950408889634
D = 1152
ROWS = 64
HALF = 32
TILE = 1024

CLIP_BLOCK = {0: 0, 1: 1, 3: 2, 2: 3}
TEXT_GROUP = {4: 0, 0: 1, 3: 2, 5: 3, 2: 4, 6: 5, 1: 6, 7: 7}


def clip_at(half, apart, index):
    return CLIP_BLOCK[apart] * 256 + half * 128 + index * HALF


def text_at(dz, dk):
    return TEXT_GROUP[dz] * 128 + dk * ROWS


def kernel(
    clip_ref, text_ref, pos_ref, log_temp_ref, bias_ref,
    grad_clip_ref, grad_text_ref, loss_ref, grad_temp_ref, grad_bias_ref,
    clu, txu, posb, posc, colid, dl, gc, gt, acc,
    cs1, cr1, cs2, cr2, cs3, cr3, ks, kr, zs, zr, sums, sumr,
    clip_send, clip_recv, text_send, text_recv, core_send, core_recv, pos_send, pos_recv,
    c1_send, c1_recv, c2_send, c2_recv, c3_send, c3_recv, k_send, k_recv, z_send, z_recv, s_send, s_recv,
):
    c = lax.axis_index("clip")
    t = lax.axis_index("text")
    x, y, z, k = t // 4, c // 4, (t % 4) * 2 + (c // 2) % 2, c % 2

    def dev(dx=0, dy=0, dz=0, dk=0):
        ax, ay, az, ak = (x + dx) % 4, (y + dy) % 4, (z + dz) % 8, (k + dk) % 2
        return (ay * 4 + (az % 2) * 2 + ak, ax * 4 + az // 2)

    def along(half, step):
        return dev(dy=step) if half == 0 else dev(dx=step)

    def across(half, step):
        return dev(dx=step) if half == 0 else dev(dy=step)

    started = []

    def send(src, dst, ssem, rsem, to):
        copy = pltpu.make_async_remote_copy(
            src_ref=src, dst_ref=dst, send_sem=ssem, recv_sem=rsem, device_id=to, device_id_type=MESH
        )
        copy.start()
        started.append(copy)
        return copy

    peers = [dev(dx=i) for i in (1, 2, 3)] + [dev(dy=i) for i in (1, 2, 3)]
    peers += [dev(dz=i) for i in range(1, 8)] + [dev(dk=1)]
    barrier = pltpu.get_barrier_semaphore()
    for peer in peers:
        pl.semaphore_signal(barrier, inc=1, device_id=peer, device_id_type=MESH)

    def unit_rows(ref):
        wide = ref[...].astype(F32)
        scale = lax.rsqrt(jnp.sum(wide * wide, axis=1, keepdims=True) + 1e-06)
        return scale, wide * scale

    clip_unit = unit_rows(clip_ref)[1].astype(BF16)
    for half in (0, 1):
        clu[pl.ds(clip_at(half, 0, 0), HALF), :] = clip_unit[half * HALF:(half + 1) * HALF, :]
    txu[pl.ds(text_at(0, 0), ROWS), :] = unit_rows(text_ref)[1].astype(BF16)
    posb[0] = pos_ref[...]

    pl.semaphore_wait(barrier, len(peers))

    def text_piece(dz, dk, half):
        return txu.at[pl.ds(text_at(dz, dk) + half * HALF, HALF)]

    text_copy = {}

    def text_hop(src_dz, step, half):
        dst_dz = (src_dz - step) % 8
        text_copy[dst_dz, half] = send(
            text_piece(src_dz, 0, half), text_piece(dst_dz, 0, half),
            text_send.at[dst_dz, half], text_recv.at[dst_dz, half], dev(dz=step),
        )

    core_copy = {}

    def text_core(dz):
        rows = pl.ds(text_at(dz, 0), ROWS)
        core_copy[dz] = send(
            txu.at[rows], txu.at[pl.ds(text_at(dz, 1), ROWS)], core_send.at[dz], core_recv.at[dz], dev(dk=1)
        )

    clip_copy = {}

    def clip_piece(half, apart, index):
        return clu.at[pl.ds(clip_at(half, apart, index), HALF)]

    def clip_first(half, step):
        index = (-step) % 4
        clip_copy[half, 0, index] = send(
            clip_piece(half, 0, 0), clip_piece(half, 0, index),
            clip_send.at[half, 0, index], clip_recv.at[half, 0, index], across(half, step),
        )

    def clip_second(half, src_apart, index, step):
        apart = (src_apart - step) % 4
        clip_copy[half, apart, index] = send(
            clip_piece(half, src_apart, index), clip_piece(half, apart, index),
            clip_send.at[half, apart, index], clip_recv.at[half, apart, index], along(half, step),
        )

    for step in (1, -1, 2):
        for half in (0, 1):
            clip_first(half, step)
    for half in (0, 1):
        text_hop(0, 1, half)
        text_hop(0, -1, 1 - half)
    for half in (0, 1):
        clip_second(half, 0, 0, 1)
        clip_second(half, 0, 0, -1)
    text_core(0)
    pos_copy = [
        send(posb.at[0], posb.at[(-step) % 4], pos_send.at[step], pos_recv.at[step], dev(dy=step)) for step in (1, 2, 3)
    ]

    lane = lax.broadcasted_iota(jnp.int32, (8, 128), 1)
    for dz in range(8):
        az = (z + dz) % 8
        base = (x * 4 + az // 2) * 1024 + (y * 4 + (az % 2) * 2) * ROWS
        ids = jnp.where(lane < ROWS, base + k * ROWS, base + (1 - k) * ROWS) + lane % ROWS
        colid[:, pl.ds(text_at(dz, 0), 128)] = ids.astype(F32)

    order = {0: (1, 3, 2), 1: (1, 3, 2)}
    for index in order[0]:
        for half in (0, 1):
            clip_copy[half, 0, index].wait_recv()
            clip_second(half, 0, index, 1 if index < 2 else -1)
            clip_second(half, 0, index, -1 if index < 2 else 1)
    for dz, step in ((7, 1), (1, -1)):
        for half in (0, 1) if step == 1 else (1, 0):
            text_copy[dz, half].wait_recv()
            text_hop(dz, step, half)
        text_core(dz)
    for half in (0, 1):
        for index in (0, 1):
            clip_copy[half, 3, index].wait_recv()
            clip_second(half, 3, index, 1)
        for index in (3, 2):
            clip_copy[half, 1, index].wait_recv()
            clip_second(half, 1, index, -1)
    for dz, step in ((6, 1), (2, -1)):
        for half in (0, 1) if step == 1 else (1, 0):
            text_copy[dz, half].wait_recv()
            text_hop(dz, step, half)
        text_core(dz)

    for copy in pos_copy:
        copy.wait_recv()
    z_hi = z // 2
    row_in = lax.broadcasted_iota(jnp.int32, (HALF, 128), 0)
    lane_in = lax.broadcasted_iota(jnp.int32, (HALF, 128), 1)
    for half in (0, 1):
        hit = lane_in == row_in + ((z_hi % 2) * ROWS + half * HALF)
        for dx in range(4):
            for dy in range(4):
                apart, index = (dy, dx) if half == 0 else (dx, dy)
                row = ((x + dx) % 4) * 2 + z_hi // 2
                values = posb[dy, pl.ds(row, 1), :].astype(F32)
                posc[pl.ds(clip_at(half, apart, index), HALF), :] = jnp.sum(
                    jnp.where(hit, values, 0.0), axis=1, keepdims=True
                )

    for dz, step in ((5, 1), (3, -1)):
        for half in (0, 1) if step == 1 else (1, 0):
            text_copy[dz, half].wait_recv()
            if half == (0 if step == 1 else 1):
                text_hop(dz, step, half)
        text_core(dz)
    for half in (0, 1):
        text_copy[4, half].wait_recv()
    text_core(4)
    for half in (0, 1):
        for index in (2, 3):
            clip_copy[half, 3, index].wait_recv()
        for index in (0, 1):
            clip_copy[half, 1, index].wait_recv()
        for index in range(4):
            clip_copy[half, 2, index].wait_recv()
    for dz in range(8):
        core_copy[dz].wait_recv()

    temp = jnp.exp(jnp.full((8, 128), log_temp_ref[0, 0], F32))
    factor = (temp * LOG2E)[0:1, 0:1]
    offset = bias_ref[0, 0] * LOG2E
    acc[...] = jnp.zeros_like(acc)

    def fold(value):
        return jnp.sum(value.reshape(32, 8, 8, 128), axis=(0, 2))

    def block(i, carry):
        rows = pl.ds(pl.multiple_of(i * 256, 256), 256)
        sims = lax.dot_general(clu[rows, :], txu[...], (((1,), (1,)), ((), ())), preferred_element_type=F32)
        e = jnp.exp2(sims * factor + offset)
        plus = 1.0 + e
        inverse = 1.0 / plus
        mask = posc[rows, :] == colid[0:1, :]
        dlogit = jnp.where(mask, -inverse, e * inverse)
        acc[0] += fold(jnp.log(plus))
        acc[1] += fold(dlogit)
        acc[2] += fold(dlogit * sims)
        acc[3] += fold(jnp.where(mask, sims, 0.0))
        dl[rows, :] = dlogit.astype(BF16)
        return carry

    lax.fori_loop(0, 4, block, 0)

    sum_copy = []

    def share(slots, targets):
        copies = [
            send(sums.at[slots[0]], sumr.at[slot], s_send.at[slot], s_recv.at[slot], to)
            for slot, to in zip(slots, targets)
        ]
        return copies

    def collect(copies, slots, nxt):
        total = sums[slots[0]]
        for copy, slot in zip(copies, slots):
            copy.wait_recv()
            total = total + sumr[slot]
        sums[nxt] = total

    for i in range(4):
        sums[0, pl.ds(i, 1), :] = jnp.sum(acc[i], axis=0, keepdims=True)
    sums[0, pl.ds(4, 4), :] = jnp.zeros((4, 128), F32)
    core_slots, x_slots, y_slots, z_slots = (0,), (1, 2, 3), (4, 5, 6), tuple(range(7, 14))
    core_share = share(core_slots, [dev(dk=1)])

    def text_grad(i):
        rows = pl.ds(i * 256, 256)
        gt[rows, :] = lax.dot_general(dl[:, i * 256:(i + 1) * 256], clu[...], (((0,), (0,)), ((), ())), preferred_element_type=F32)

    def clip_grad(i):
        rows = pl.ds(i * 256, 256)
        gc[rows, :] = lax.dot_general(dl[rows, :], txu[...], (((1,), (0,)), ((), ())), preferred_element_type=F32)

    k_copy = {}

    def to_core(dz):
        ks[dz] = gt[pl.ds(text_at(dz, 1), ROWS), :].astype(BF16)
        k_copy[dz] = send(ks.at[dz], kr.at[dz], k_send.at[dz], k_recv.at[dz], dev(dk=1))

    def text_sum(dz, half):
        return gt[pl.ds(text_at(dz, 0) + half * HALF, HALF), :] + kr[dz, pl.ds(half * HALF, HALF), :].astype(F32)

    z_copy = {}

    def ring(way, stage, half, dz):
        part = pl.ds(half * HALF, HALF)
        value = text_sum(dz, half)
        if (way, stage - 1, half) in z_copy:
            z_copy[way, stage - 1, half].wait_recv()
            value = value + zr[way, stage - 1, part, :].astype(F32)
        zs[dz, part, :] = value.astype(BF16)
        z_copy[way, stage, half] = send(
            zs.at[dz, part], zr.at[way, stage, part], z_send.at[way, stage, half], z_recv.at[way, stage, half],
            dev(dz=1 if way == 0 else -1),
        )

    c1_copy = {}
    c2_copy = {}
    c3_copy = {}

    def clip_r1(half):
        for index in range(4):
            cs1[half, index] = gc[pl.ds(clip_at(half, 2, index), HALF), :].astype(BF16)
            c1_copy[half, index] = send(
                cs1.at[half, index], cr1.at[half, index], c1_send.at[half, index], c1_recv.at[half, index],
                along(half, 1 if index < 2 else -1),
            )

    def clip_r2(half, way):
        apart = 1 if way == 0 else 3
        passed = (0, 1) if way == 0 else (2, 3)
        for index in (2, 3, 0, 1) if way == 0 else (0, 1, 2, 3):
            value = gc[pl.ds(clip_at(half, apart, index), HALF), :]
            if index in passed:
                c1_copy[half, index].wait_recv()
                value = value + cr1[half, index].astype(F32)
            cs2[half, way, index] = value.astype(BF16)
            c2_copy[half, way, index] = send(
                cs2.at[half, way, index], cr2.at[half, way, index],
                c2_send.at[half, way, index], c2_recv.at[half, way, index],
                along(half, 1 if way == 0 else -1),
            )

    def clip_r3(half):
        for index in (2, 1, 3, 0):
            value = gc[pl.ds(clip_at(half, 0, index), HALF), :]
            for way in (0, 1):
                c2_copy[half, way, index].wait_recv()
                value = value + cr2[half, way, index].astype(F32)
            if index == 0:
                gc[pl.ds(clip_at(half, 0, 0), HALF), :] = value
            else:
                cs3[half, index - 1] = value.astype(BF16)
                c3_copy[half, index] = send(
                    cs3.at[half, index - 1], cr3.at[half, index - 1],
                    c3_send.at[half, index - 1], c3_recv.at[half, index - 1], across(half, index),
                )

    text_grad(0)
    to_core(4)
    text_grad(1)
    to_core(3)
    to_core(5)
    clip_grad(3)
    clip_r1(0)
    clip_r1(1)
    collect(core_share, core_slots, 1)
    x_share = share(x_slots, [dev(dx=i) for i in (1, 2, 3)])
    k_copy[4].wait_recv()
    ring(0, 0, 0, 4)
    ring(1, 0, 1, 4)
    text_grad(2)
    to_core(2)
    to_core(6)
    k_copy[3].wait_recv()
    k_copy[5].wait_recv()
    ring(0, 1, 1, 3)
    ring(1, 1, 0, 5)
    clip_grad(1)
    clip_grad(2)
    for half in (0, 1):
        clip_r2(half, 0)
        clip_r2(half, 1)
    ring(0, 1, 0, 3)
    ring(1, 1, 1, 5)
    text_grad(3)
    to_core(1)
    to_core(7)
    to_core(0)
    k_copy[2].wait_recv()
    k_copy[6].wait_recv()
    collect(x_share, x_slots, 4)
    y_share = share(y_slots, [dev(dy=i) for i in (1, 2, 3)])
    clip_grad(0)
    for half in (1, 0):
        ring(0, 2, half, 2)
        ring(1, 2, 1 - half, 6)
    for half in (0, 1):
        clip_r3(half)
    collect(y_share, y_slots, 7)
    z_share = share(z_slots, [dev(dz=i) for i in range(1, 8)])
    k_copy[1].wait_recv()
    k_copy[7].wait_recv()
    for half in (1, 0):
        ring(0, 3, half, 1)
        ring(1, 3, 1 - half, 7)

    def finish(scale, normal, back):
        return scale * (back - normal * jnp.sum(normal * back, axis=1, keepdims=True))

    temp_one = temp[0:1, 0:1]
    clip_scale, clip_norm = unit_rows(clip_ref)
    for half in (0, 1):
        value = gc[pl.ds(clip_at(half, 0, 0), HALF), :]
        for index in (1, 2, 3):
            c3_copy[half, index].wait_recv()
            value = value + cr3[half, index - 1].astype(F32)
        part = slice(half * HALF, (half + 1) * HALF)
        grad_clip_ref[part, :] = finish(clip_scale[part], clip_norm[part], temp_one * value)
    k_copy[0].wait_recv()
    text_scale, text_norm = unit_rows(text_ref)
    for half in (0, 1):
        value = text_sum(0, half)
        for way in (0, 1):
            z_copy[way, 3, half].wait_recv()
            value = value + zr[way, 3, pl.ds(half * HALF, HALF), :].astype(F32)
        part = slice(half * HALF, (half + 1) * HALF)
        grad_text_ref[part, :] = finish(text_scale[part], text_norm[part], temp_one * value)

    collect(z_share, z_slots, 14)
    total = sums[14]
    pairs = 16384.0
    log_sum = jnp.sum(total[0:1, :])
    bias_sum = jnp.sum(total[1:2, :])
    temp_sum = jnp.sum(total[2:3, :])
    positive_sum = jnp.sum(total[3:4, :])
    temp_scalar = jnp.sum(jnp.where(lane == 0, temp, 0.0)[0:1, :])
    loss_ref[0, 0] = (log_sum - temp_scalar * positive_sum) / pairs - bias_ref[0, 0]
    grad_temp_ref[0, 0] = temp_scalar * temp_sum / pairs
    grad_bias_ref[0, 0] = bias_sum / pairs

    for copy in started:
        copy.wait_send()


def per_device(clip_emb, text_emb, positive, log_temp, bias):
    vmem = pl.BlockSpec(memory_space=pltpu.VMEM)
    smem = pl.BlockSpec(memory_space=pltpu.SMEM)
    one = jax.ShapeDtypeStruct((1, 1), F32)
    rows = jax.ShapeDtypeStruct((ROWS, D), F32)
    dma = pltpu.SemaphoreType.DMA
    grad_clip, grad_text, loss, grad_temp, grad_bias = pl.pallas_call(
        kernel,
        out_shape=(rows, rows, one, one, one),
        in_specs=[vmem, vmem, vmem, smem, smem],
        out_specs=(vmem, vmem, smem, smem, smem),
        scratch_shapes=[
            pltpu.VMEM((TILE, D), BF16),
            pltpu.VMEM((TILE, D), BF16),
            pltpu.VMEM((4, 8, 128), jnp.int32),
            pltpu.VMEM((TILE, 1), F32),
            pltpu.VMEM((8, TILE), F32),
            pltpu.VMEM((TILE, TILE), BF16),
            pltpu.VMEM((TILE, D), F32),
            pltpu.VMEM((TILE, D), F32),
            pltpu.VMEM((4, 8, 128), F32),
            pltpu.VMEM((2, 4, HALF, D), BF16),
            pltpu.VMEM((2, 4, HALF, D), BF16),
            pltpu.VMEM((2, 2, 4, HALF, D), BF16),
            pltpu.VMEM((2, 2, 4, HALF, D), BF16),
            pltpu.VMEM((2, 3, HALF, D), BF16),
            pltpu.VMEM((2, 3, HALF, D), BF16),
            pltpu.VMEM((8, ROWS, D), BF16),
            pltpu.VMEM((8, ROWS, D), BF16),
            pltpu.VMEM((8, ROWS, D), BF16),
            pltpu.VMEM((2, 4, ROWS, D), BF16),
            pltpu.VMEM((15, 8, 128), F32),
            pltpu.VMEM((14, 8, 128), F32),
            dma((2, 4, 4)), dma((2, 4, 4)), dma((8, 2)), dma((8, 2)), dma((8,)), dma((8,)), dma((4,)), dma((4,)),
            dma((2, 4)), dma((2, 4)), dma((2, 2, 4)), dma((2, 2, 4)), dma((2, 3)), dma((2, 3)),
            dma((8,)), dma((8,)), dma((2, 4, 2)), dma((2, 4, 2)), dma((14,)), dma((14,)),
        ],
        compiler_params=pltpu.CompilerParams(
            collective_id=0, has_side_effects=True, vmem_limit_bytes=50 * 2**20
        ),
        cost_estimate=pl.CostEstimate(flops=7247757312, bytes_accessed=900000, transcendentals=3 * 2**20),
    )(clip_emb, text_emb[0], positive.reshape(8, 128), log_temp.reshape(1, 1), bias.reshape(1, 1))
    return (
        loss.reshape(()), grad_clip, grad_text[None], grad_temp.reshape(()), grad_bias.reshape(()),
    )


def solution(mesh):
    return jax.shard_map(
        per_device,
        mesh=mesh,
        in_specs=(P(("clip", "text"), None), P("text", "clip", None), P("clip"), P(), P()),
        out_specs=(P(), P(("clip", "text"), None), P("text", "clip", None), P(), P()),
        check_vma=False,
    )
```

```python
import jax
import jax.numpy as jnp
from jax import lax
from jax.experimental import pallas as pl
from jax.experimental.pallas import tpu as pltpu
from jax.sharding import PartitionSpec as P

MESH = pl.DeviceIdType.MESH
F32 = jnp.float32
BF16 = jnp.bfloat16
LOG2E = 1.4426950408889634
D = 1152
ROWS = 64
HALF = 32
TILE = 1024

CLIP_BLOCK = {0: 0, 1: 1, 3: 2, 2: 3}
TEXT_GROUP = {0: 0, 1: 1, 7: 2, 2: 3, 6: 4, 3: 5, 5: 6, 4: 7}
CHUNK = 16
PARTS = ROWS // CHUNK


def clip_at(half, apart, index):
    return CLIP_BLOCK[apart] * 256 + half * 128 + index * HALF


def text_at(dz, dk):
    return TEXT_GROUP[dz] * 128 + dk * ROWS


def kernel(
    clip_hbm, text_hbm, pos_hbm, log_temp_hbm, bias_hbm,
    grad_clip_ref, grad_text_ref, scalar_ref,
    clip_ref, text_ref, log_temp_ref, bias_ref, clip_norm, clip_scale, text_norm, text_scale,
    clu, txu, posb, posc, colid, dl, gc, gt, acc,
    cs1, cr1, cs2, cr2, cs3, cr3, ks, kr, zs, zr, sums, sumr,
    in_sem,
    clip_send, clip_recv, text_send, text_recv, core_send, core_recv, pos_send, pos_recv,
    c1_send, c1_recv, c2_send, c2_recv, c3_send, c3_recv, k_send, k_recv, z_send, z_recv, s_send, s_recv,
):
    c = lax.axis_index("clip")
    t = lax.axis_index("text")
    x, y, z, k = t // 4, c // 4, (t % 4) * 2 + (c // 2) % 2, c % 2

    def dev(dx=0, dy=0, dz=0, dk=0):
        ax, ay, az, ak = (x + dx) % 4, (y + dy) % 4, (z + dz) % 8, (k + dk) % 2
        return (ay * 4 + (az % 2) * 2 + ak, ax * 4 + az // 2)

    def along(half, step):
        return dev(dy=step) if half == 0 else dev(dx=step)

    def across(half, step):
        return dev(dx=step) if half == 0 else dev(dy=step)

    started = []

    def send(src, dst, ssem, rsem, to):
        copy = pltpu.make_async_remote_copy(
            src_ref=src, dst_ref=dst, send_sem=ssem, recv_sem=rsem, device_id=to, device_id_type=MESH
        )
        copy.start()
        started.append(copy)
        return copy

    peers = [dev(dx=i) for i in (1, 2, 3)] + [dev(dy=i) for i in (1, 2, 3)]
    peers += [dev(dz=i) for i in (1, 7)] + [dev(dk=1)]
    barrier = pltpu.get_barrier_semaphore()
    for peer in peers:
        pl.semaphore_signal(barrier, inc=1, device_id=peer, device_id_type=MESH)
    loads = [
        pltpu.make_async_copy(src, dst, in_sem.at[i])
        for i, (src, dst) in enumerate(
            [(clip_hbm, clip_ref), (text_hbm, text_ref), (pos_hbm, posb.at[0]), (log_temp_hbm, log_temp_ref), (bias_hbm, bias_ref)]
        )
    ]
    for load in loads:
        load.start()

    def unit_rows(ref, scale_ref, norm_ref):
        wide = ref[...].astype(F32)
        scale = lax.rsqrt(jnp.sum(wide * wide, axis=1, keepdims=True) + 1e-06)
        normal = wide * scale
        scale_ref[...] = scale
        norm_ref[...] = normal
        return normal.astype(BF16)

    loads[0].wait()
    clip_unit = unit_rows(clip_ref, clip_scale, clip_norm)
    for half in (0, 1):
        clu[pl.ds(clip_at(half, 0, 0), HALF), :] = clip_unit[half * HALF:(half + 1) * HALF, :]
    loads[1].wait()
    txu[pl.ds(text_at(0, 0), ROWS), :] = unit_rows(text_ref, text_scale, text_norm)
    for load in loads[2:]:
        load.wait()

    pl.semaphore_wait(barrier, len(peers))

    def text_piece(dz, dk, part):
        return txu.at[pl.ds(text_at(dz, dk) + part * CHUNK, CHUNK)]

    text_copy = {}

    def text_hop(src_dz, step, part):
        dst_dz = (src_dz - step) % 8
        text_copy[dst_dz, part] = send(
            text_piece(src_dz, 0, part), text_piece(dst_dz, 0, part),
            text_send.at[dst_dz, part], text_recv.at[dst_dz, part], dev(dz=step),
        )

    core_copy = {}

    def text_core(dz):
        rows = pl.ds(text_at(dz, 0), ROWS)
        core_copy[dz] = [
            send(txu.at[rows], txu.at[pl.ds(text_at(dz, 1), ROWS)], core_send.at[dz], core_recv.at[dz], dev(dk=1))
        ]

    def core_part(dz, half):
        mine, other = [pl.ds(text_at(dz, dk) + half * HALF, HALF) for dk in (0, 1)]
        copy = send(txu.at[mine], txu.at[other], core_send.at[dz + half * 4], core_recv.at[dz + half * 4], dev(dk=1))
        core_copy.setdefault(dz, []).append(copy)

    clip_copy = {}

    def clip_piece(half, apart, index):
        return clu.at[pl.ds(clip_at(half, apart, index), HALF)]

    def clip_first(half, step):
        index = (-step) % 4
        clip_copy[half, 0, index] = send(
            clip_piece(half, 0, 0), clip_piece(half, 0, index),
            clip_send.at[half, 0, index], clip_recv.at[half, 0, index], across(half, step),
        )

    def clip_second(half, src_apart, index, step):
        apart = (src_apart - step) % 4
        clip_copy[half, apart, index] = send(
            clip_piece(half, src_apart, index), clip_piece(half, apart, index),
            clip_send.at[half, apart, index], clip_recv.at[half, apart, index], along(half, step),
        )

    def text_step(distance, part):
        for step in (1, -1):
            dz = -distance % 8 if step == 1 else distance
            at = part if step == 1 else PARTS - 1 - part
            text_copy[dz, at].wait_recv()
            if distance < 3 or (distance == 3 and part < PARTS // 2):
                text_hop(dz, step, at)
            if distance == 4:
                if part == PARTS // 2 - 1:
                    core_part(4, 0 if step == 1 else 1)
            elif part == PARTS - 1:
                text_core(dz)

    def clip_pass(index):
        for half in (0, 1):
            clip_copy[half, 0, index].wait_recv()
            for step in (1, -1) if index < 2 else (-1, 1):
                clip_second(half, 0, index, step)

    def clip_on(index):
        for half in (0, 1):
            if index < 2:
                clip_copy[half, 3, index].wait_recv()
                clip_second(half, 3, index, 1)
            else:
                clip_copy[half, 1, index].wait_recv()
                clip_second(half, 1, index, -1)

    def clip_near():
        for half in (0, 1):
            for index in range(4):
                clip_copy[half, 1 if index < 2 else 3, index].wait_recv()

    def clip_far():
        for half in (0, 1):
            for index in range(4):
                clip_copy[half, 2, index].wait_recv()

    for part in range(PARTS):
        text_hop(0, 1, part)
        text_hop(0, -1, PARTS - 1 - part)
    for step in (1, -1, 2):
        for half in (0, 1):
            clip_first(half, step)
    for half in (0, 1):
        clip_second(half, 0, 0, 1)
        clip_second(half, 0, 0, -1)
    text_core(0)
    pos_copy = [
        send(posb.at[0], posb.at[(-step) % 4], pos_send.at[step], pos_recv.at[step], dev(dy=step)) for step in (1, 2, 3)
    ]

    lane = lax.broadcasted_iota(jnp.int32, (8, 128), 1)
    for dz in range(8):
        az = (z + dz) % 8
        base = (x * 4 + az // 2) * 1024 + (y * 4 + (az % 2) * 2) * ROWS
        ids = jnp.where(lane < ROWS, base + k * ROWS, base + (1 - k) * ROWS) + lane % ROWS
        colid[:, pl.ds(text_at(dz, 0), 128)] = ids.astype(F32)
    temp = jnp.exp(jnp.broadcast_to(log_temp_ref[...], (8, 128)))
    factor = (temp * LOG2E)[0:1, 0:1]
    offset = bias_ref[...] * LOG2E
    acc[...] = jnp.zeros_like(acc)

    def fold(value):
        rows, columns = value.shape
        return jnp.sum(value.reshape(rows // 8, 8, columns // 128, 128), axis=(0, 2))

    def piece(block, first, last):
        rows = pl.ds(block * 256, 256)
        columns = pl.ds(first * 128, (last - first) * 128)
        sims = lax.dot_general(clu[rows, :], txu[columns, :], (((1,), (1,)), ((), ())), preferred_element_type=F32)
        e = jnp.exp2(sims * factor + offset)
        plus = 1.0 + e
        inverse = 1.0 / plus
        mask = posc[rows, :] == colid[0:1, columns]
        dlogit = jnp.where(mask, -inverse, e * inverse)
        acc[0] += fold(jnp.log(plus))
        acc[1] += fold(dlogit)
        acc[2] += fold(dlogit * sims)
        acc[3] += fold(jnp.where(mask, sims, 0.0))
        dl[rows, columns] = dlogit.astype(BF16)

    def positives():
        for copy in pos_copy:
            copy.wait_recv()
        z_hi = z // 2
        row_in = lax.broadcasted_iota(jnp.int32, (HALF, 128), 0)
        lane_in = lax.broadcasted_iota(jnp.int32, (HALF, 128), 1)
        for half in (0, 1):
            hit = lane_in == row_in + ((z_hi % 2) * ROWS + half * HALF)
            for dx in range(4):
                for dy in range(4):
                    apart, index = (dy, dx) if half == 0 else (dx, dy)
                    row = ((x + dx) % 4) * 2 + z_hi // 2
                    values = posb[dy, pl.ds(row, 1), :].astype(F32)
                    posc[pl.ds(clip_at(half, apart, index), HALF), :] = jnp.sum(
                        jnp.where(hit, values, 0.0), axis=1, keepdims=True
                    )

    def text_ready(*groups):
        for dz in groups:
            for copy in core_copy[dz]:
                copy.wait_recv()

    text_step(1, 0)
    clip_pass(1)
    clip_pass(3)
    text_step(1, 1)
    text_step(1, 2)
    clip_pass(2)
    text_step(1, 3)
    positives()
    text_step(2, 0)
    clip_on(0)
    clip_on(3)
    text_step(2, 1)
    text_step(2, 2)
    clip_on(1)
    clip_on(2)
    text_step(2, 3)
    text_ready(0, 1, 7, 2)
    piece(0, 0, 4)
    text_step(3, 0)
    text_step(3, 1)
    clip_near()
    piece(1, 0, 4)
    text_step(3, 2)
    text_step(3, 3)
    piece(2, 0, 4)
    text_ready(6, 3, 5)
    piece(0, 4, 7)
    text_step(4, 0)
    piece(1, 4, 7)
    piece(2, 4, 7)
    text_step(4, 1)
    clip_far()
    piece(3, 0, 4)
    text_ready(4)
    piece(3, 4, 8)
    for i in range(3):
        piece(i, 7, 8)

    def share(slots, targets):
        return [
            send(sums.at[slots[0]], sumr.at[slot], s_send.at[slot], s_recv.at[slot], to)
            for slot, to in zip(slots, targets)
        ]

    def collect(copies, slots, nxt):
        total = sums[slots[0]]
        for copy, slot in zip(copies, slots):
            copy.wait_recv()
            total = total + sumr[slot]
        sums[nxt] = total

    for i in range(4):
        sums[0, pl.ds(i, 1), :] = jnp.sum(acc[i], axis=0, keepdims=True)
    sums[0, pl.ds(4, 4), :] = jnp.zeros((4, 128), F32)
    core_slots, x_slots, y_slots, z_slots = (0,), (1, 2, 3), (4, 5, 6), tuple(range(7, 14))
    core_share = share(core_slots, [dev(dk=1)])

    def text_grad(i):
        rows = pl.ds(i * 256, 256)
        gt[rows, :] = lax.dot_general(dl[:, i * 256:(i + 1) * 256], clu[...], (((0,), (0,)), ((), ())), preferred_element_type=F32)

    def clip_grad(i):
        rows = pl.ds(i * 256, 256)
        gc[rows, :] = lax.dot_general(dl[rows, :], txu[...], (((1,), (0,)), ((), ())), preferred_element_type=F32)

    k_copy = {}

    def to_core(dz):
        ks[dz] = gt[pl.ds(text_at(dz, 1), ROWS), :].astype(BF16)
        k_copy[dz] = send(ks.at[dz], kr.at[dz], k_send.at[dz], k_recv.at[dz], dev(dk=1))

    def text_sum(dz, part):
        rows = pl.ds(part * CHUNK, CHUNK)
        return gt[pl.ds(text_at(dz, 0) + part * CHUNK, CHUNK), :] + kr[dz, rows, :].astype(F32)

    z_copy = {}

    def ring(stage, part):
        for way in (0, 1):
            dz = 4 - stage if way == 0 else 4 + stage
            at = part if way == 0 else PARTS - 1 - part
            rows = pl.ds(at * CHUNK, CHUNK)
            value = text_sum(dz, at)
            if stage > 1 or (stage == 1 and part < PARTS // 2):
                z_copy[way, stage - 1, at].wait_recv()
                value = value + zr[way, stage - 1, rows, :].astype(F32)
            zs[dz, rows, :] = value.astype(BF16)
            z_copy[way, stage, at] = send(
                zs.at[dz, rows], zr.at[way, stage, rows], z_send.at[way, stage, at], z_recv.at[way, stage, at],
                dev(dz=1 if way == 0 else -1),
            )

    def core_back(dz):
        k_copy[dz].wait_recv()

    c1_copy = {}
    c2_copy = {}
    c3_copy = {}

    def clip_r1(*indices):
        for index in indices:
            for half in (0, 1):
                cs1[half, index] = gc[pl.ds(clip_at(half, 2, index), HALF), :].astype(BF16)
                c1_copy[half, index] = send(
                    cs1.at[half, index], cr1.at[half, index], c1_send.at[half, index], c1_recv.at[half, index],
                    along(half, 1 if index < 2 else -1),
                )

    def clip_r2(way, *indices):
        apart = 1 if way == 0 else 3
        for index in indices:
            for half in (0, 1):
                value = gc[pl.ds(clip_at(half, apart, index), HALF), :]
                if (index < 2) == (way == 0):
                    c1_copy[half, index].wait_recv()
                    value = value + cr1[half, index].astype(F32)
                cs2[half, way, index] = value.astype(BF16)
                c2_copy[half, way, index] = send(
                    cs2.at[half, way, index], cr2.at[half, way, index],
                    c2_send.at[half, way, index], c2_recv.at[half, way, index],
                    along(half, 1 if way == 0 else -1),
                )

    def clip_r3(index):
        for half in (0, 1):
            value = gc[pl.ds(clip_at(half, 0, index), HALF), :]
            for way in (0, 1):
                c2_copy[half, way, index].wait_recv()
                value = value + cr2[half, way, index].astype(F32)
            if index == 0:
                gc[pl.ds(clip_at(half, 0, 0), HALF), :] = value
            else:
                cs3[half, index - 1] = value.astype(BF16)
                c3_copy[half, index] = send(
                    cs3.at[half, index - 1], cr3.at[half, index - 1],
                    c3_send.at[half, index - 1], c3_recv.at[half, index - 1], across(half, index),
                )

    text_grad(3)
    to_core(4)
    to_core(5)
    clip_grad(3)
    clip_r1(1, 2)
    clip_r1(0, 3)
    core_back(4)
    ring(0, 0)
    ring(0, 1)
    text_grad(2)
    to_core(3)
    to_core(6)
    clip_grad(1)
    clip_r2(0, 2, 3)
    clip_grad(2)
    clip_r2(1, 1, 0)
    core_back(3)
    core_back(5)
    ring(1, 2)
    ring(1, 3)
    collect(core_share, core_slots, 1)
    x_share = share(x_slots, [dev(dx=i) for i in (1, 2, 3)])
    text_grad(1)
    to_core(2)
    to_core(7)
    ring(1, 0)
    clip_r2(0, 1)
    clip_r2(1, 2)
    ring(1, 1)
    text_grad(0)
    to_core(1)
    to_core(0)
    clip_r2(0, 0)
    clip_r2(1, 3)
    clip_grad(0)
    core_back(2)
    core_back(6)
    ring(2, 2)
    ring(2, 3)
    collect(x_share, x_slots, 4)
    y_share = share(y_slots, [dev(dy=i) for i in (1, 2, 3)])
    ring(2, 0)
    clip_r3(2)
    clip_r3(1)
    ring(2, 1)
    clip_r3(3)
    clip_r3(0)
    core_back(1)
    core_back(7)
    ring(3, 2)
    ring(3, 3)
    ring(3, 0)
    ring(3, 1)
    collect(y_share, y_slots, 7)
    z_share = share(z_slots, [dev(dz=i) for i in range(1, 8)])
    core_back(0)

    def finish(scale, normal, back):
        return scale * (back - normal * jnp.sum(normal * back, axis=1, keepdims=True))

    temp_one = temp[0:1, 0:1]

    def finish_text(part):
        rows = pl.ds(part * CHUNK, CHUNK)
        value = text_sum(0, part)
        for way in (0, 1):
            z_copy[way, 3, part].wait_recv()
            value = value + zr[way, 3, rows, :].astype(F32)
        grad_text_ref[rows, :] = finish(text_scale[rows, :], text_norm[rows, :], temp_one * value)

    def finish_clip(half):
        rows = pl.ds(half * HALF, HALF)
        value = gc[pl.ds(clip_at(half, 0, 0), HALF), :]
        for index in (1, 3, 2):
            c3_copy[half, index].wait_recv()
            value = value + cr3[half, index - 1].astype(F32)
        grad_clip_ref[rows, :] = finish(clip_scale[rows, :], clip_norm[rows, :], temp_one * value)

    for half in (0, 1):
        finish_clip(half)
    for part in range(PARTS):
        finish_text(part)
    collect(z_share, z_slots, 14)

    total = jnp.sum(sums[14], axis=1, keepdims=True)
    pairs = 16384.0
    loss = (total[0:1] - temp_one * total[3:4]) / pairs - bias_ref[...]
    for i, value in enumerate((loss, temp_one * total[2:3] / pairs, total[1:2] / pairs)):
        scalar_ref[pl.ds(i, 1), :] = jnp.broadcast_to(value, (1, 128))

    for copy in started:
        copy.wait_send()


def deliver(grad_clip_in, grad_text_in, scalar_in, grad_clip_ref, grad_text_ref, loss_ref, grad_temp_ref, grad_bias_ref, ones, sem):
    pairs = [(grad_clip_in, grad_clip_ref), (grad_text_in, grad_text_ref)]
    for i, ref in enumerate((loss_ref, grad_temp_ref, grad_bias_ref)):
        ones[i] = scalar_in[pl.ds(i, 1), 0:1]
        pairs.append((ones.at[i], ref))
    copies = [pltpu.make_async_copy(src, dst, sem.at[i]) for i, (src, dst) in enumerate(pairs)]
    for copy in copies:
        copy.start()
    for copy in copies:
        copy.wait()


def per_device(clip_emb, text_emb, positive, log_temp, bias):
    hbm = pl.BlockSpec(memory_space=pltpu.HBM)
    vmem = pl.BlockSpec(memory_space=pltpu.VMEM)
    one = jax.ShapeDtypeStruct((1, 1), F32)
    rows = jax.ShapeDtypeStruct((ROWS, D), F32)
    dma = pltpu.SemaphoreType.DMA
    grad_clip, grad_text, scalars = pl.pallas_call(
        kernel,
        out_shape=(rows, rows, jax.ShapeDtypeStruct((8, 128), F32)),
        in_specs=[hbm] * 5,
        out_specs=(vmem, vmem, vmem),
        scratch_shapes=[
            pltpu.VMEM((ROWS, D), BF16),
            pltpu.VMEM((ROWS, D), BF16),
            pltpu.VMEM((1, 1), F32),
            pltpu.VMEM((1, 1), F32),
            pltpu.VMEM((ROWS, D), F32),
            pltpu.VMEM((ROWS, 1), F32),
            pltpu.VMEM((ROWS, D), F32),
            pltpu.VMEM((ROWS, 1), F32),
            pltpu.VMEM((TILE, D), BF16),
            pltpu.VMEM((TILE, D), BF16),
            pltpu.VMEM((4, 8, 128), jnp.int32),
            pltpu.VMEM((TILE, 1), F32),
            pltpu.VMEM((8, TILE), F32),
            pltpu.VMEM((TILE, TILE), BF16),
            pltpu.VMEM((TILE, D), F32),
            pltpu.VMEM((TILE, D), F32),
            pltpu.VMEM((4, 8, 128), F32),
            pltpu.VMEM((2, 4, HALF, D), BF16),
            pltpu.VMEM((2, 4, HALF, D), BF16),
            pltpu.VMEM((2, 2, 4, HALF, D), BF16),
            pltpu.VMEM((2, 2, 4, HALF, D), BF16),
            pltpu.VMEM((2, 3, HALF, D), BF16),
            pltpu.VMEM((2, 3, HALF, D), BF16),
            pltpu.VMEM((8, ROWS, D), BF16),
            pltpu.VMEM((8, ROWS, D), BF16),
            pltpu.VMEM((8, ROWS, D), BF16),
            pltpu.VMEM((2, 4, ROWS, D), BF16),
            pltpu.VMEM((15, 8, 128), F32),
            pltpu.VMEM((14, 8, 128), F32),
            dma((5,)),
            dma((2, 4, 4)), dma((2, 4, 4)), dma((8, PARTS)), dma((8, PARTS)), dma((9,)), dma((9,)), dma((4,)), dma((4,)),
            dma((2, 4)), dma((2, 4)), dma((2, 2, 4)), dma((2, 2, 4)), dma((2, 3)), dma((2, 3)),
            dma((8,)), dma((8,)), dma((2, 4, PARTS)), dma((2, 4, PARTS)), dma((14,)), dma((14,)),
        ],
        compiler_params=pltpu.CompilerParams(
            collective_id=0, has_side_effects=True, vmem_limit_bytes=50 * 2**20
        ),
        cost_estimate=pl.CostEstimate(flops=7247757312, bytes_accessed=900000, transcendentals=3 * 2**20),
    )(clip_emb, text_emb[0], positive.reshape(8, 128), log_temp.reshape(1, 1), bias.reshape(1, 1))
    grad_clip, grad_text, loss, grad_temp, grad_bias = pl.pallas_call(
        deliver,
        out_shape=(rows, rows, one, one, one),
        in_specs=[vmem] * 3,
        out_specs=(hbm,) * 5,
        scratch_shapes=[pltpu.VMEM((3, 1, 1), F32), dma((5,))],
    )(grad_clip, grad_text, scalars)
    return (
        loss.reshape(()), grad_clip, grad_text[None], grad_temp.reshape(()), grad_bias.reshape(()),
    )


def solution(mesh):
    return jax.shard_map(
        per_device,
        mesh=mesh,
        in_specs=(P(("clip", "text"), None), P("text", "clip", None), P("clip"), P(), P()),
        out_specs=(P(), P(("clip", "text"), None), P("text", "clip", None), P(), P()),
        check_vma=False,
    )
```

```python
import jax
import jax.numpy as jnp
from jax import lax
from jax.experimental import pallas as pl
from jax.experimental.pallas import tpu as pltpu
from jax.sharding import PartitionSpec as P

MESH = pl.DeviceIdType.MESH
F32 = jnp.float32
BF16 = jnp.bfloat16
LOG2E = 1.4426950408889634
D = 1152
ROWS = 64
HALF = 32
TILE = 1024

CLIP_BLOCK = {0: 0, 1: 1, 3: 2, 2: 3}
TEXT_GROUP = {0: 0, 1: 1, 7: 2, 2: 3, 6: 4, 3: 5, 5: 6, 4: 7}
CHUNK = 16
PARTS = ROWS // CHUNK


def clip_at(half, apart, index):
    return CLIP_BLOCK[apart] * 256 + half * 128 + index * HALF


def text_at(dz, dk):
    return TEXT_GROUP[dz] * 128 + dk * ROWS


def kernel(
    emb_ref, pos_ref, given_ref,
    grad_clip_ref, grad_text_ref, scalar_ref,
    clip_norm, clip_scale, text_norm, text_scale,
    clu, txu, posb, posc, colid, dl, gc, gt, acc,
    cs1, cr1, cs2, cr2, cs3, cr3, ks, kr, zs, zr, sums, sumr,
    clip_send, clip_recv, text_send, text_recv, core_send, core_recv, pos_send, pos_recv,
    c1_send, c1_recv, c2_send, c2_recv, c3_send, c3_recv, k_send, k_recv, z_send, z_recv, s_send, s_recv,
):
    c = lax.axis_index("clip")
    t = lax.axis_index("text")
    x, y, z, k = t // 4, c // 4, (t % 4) * 2 + (c // 2) % 2, c % 2

    def dev(dx=0, dy=0, dz=0, dk=0):
        ax, ay, az, ak = (x + dx) % 4, (y + dy) % 4, (z + dz) % 8, (k + dk) % 2
        return (ay * 4 + (az % 2) * 2 + ak, ax * 4 + az // 2)

    def along(half, step):
        return dev(dy=step) if half == 0 else dev(dx=step)

    def across(half, step):
        return dev(dx=step) if half == 0 else dev(dy=step)

    started = []

    def send(src, dst, ssem, rsem, to):
        copy = pltpu.make_async_remote_copy(
            src_ref=src, dst_ref=dst, send_sem=ssem, recv_sem=rsem, device_id=to, device_id_type=MESH
        )
        copy.start()
        started.append(copy)
        return copy

    peers = [dev(dx=i) for i in (1, 2, 3)] + [dev(dy=i) for i in (1, 2, 3)]
    peers += [dev(dz=i) for i in (1, 7)] + [dev(dk=1)]
    barrier = pltpu.get_barrier_semaphore()
    for peer in peers:
        pl.semaphore_signal(barrier, inc=1, device_id=peer, device_id_type=MESH)
    def unit_rows(first, scale_ref, norm_ref):
        wide = emb_ref[pl.ds(first, ROWS), :].astype(F32)
        scale = lax.rsqrt(jnp.sum(wide * wide, axis=1, keepdims=True) + 1e-06)
        normal = wide * scale
        scale_ref[...] = scale
        norm_ref[...] = normal
        return normal.astype(BF16)

    clip_unit = unit_rows(0, clip_scale, clip_norm)
    for half in (0, 1):
        clu[pl.ds(clip_at(half, 0, 0), HALF), :] = clip_unit[half * HALF:(half + 1) * HALF, :]
    txu[pl.ds(text_at(0, 0), ROWS), :] = unit_rows(ROWS, text_scale, text_norm)
    posb[0] = pos_ref[...]

    pl.semaphore_wait(barrier, len(peers))

    def text_piece(dz, dk, part):
        return txu.at[pl.ds(text_at(dz, dk) + part * CHUNK, CHUNK)]

    text_copy = {}

    def text_hop(src_dz, step, part):
        dst_dz = (src_dz - step) % 8
        text_copy[dst_dz, part] = send(
            text_piece(src_dz, 0, part), text_piece(dst_dz, 0, part),
            text_send.at[dst_dz, part], text_recv.at[dst_dz, part], dev(dz=step),
        )

    core_copy = {}

    def text_core(dz):
        rows = pl.ds(text_at(dz, 0), ROWS)
        core_copy[dz] = [
            send(txu.at[rows], txu.at[pl.ds(text_at(dz, 1), ROWS)], core_send.at[dz], core_recv.at[dz], dev(dk=1))
        ]

    def core_part(dz, half):
        mine, other = [pl.ds(text_at(dz, dk) + half * HALF, HALF) for dk in (0, 1)]
        copy = send(txu.at[mine], txu.at[other], core_send.at[dz + half * 4], core_recv.at[dz + half * 4], dev(dk=1))
        core_copy.setdefault(dz, []).append(copy)

    clip_copy = {}

    def clip_piece(half, apart, index):
        return clu.at[pl.ds(clip_at(half, apart, index), HALF)]

    def clip_first(half, step):
        index = (-step) % 4
        clip_copy[half, 0, index] = send(
            clip_piece(half, 0, 0), clip_piece(half, 0, index),
            clip_send.at[half, 0, index], clip_recv.at[half, 0, index], across(half, step),
        )

    def clip_second(half, src_apart, index, step):
        apart = (src_apart - step) % 4
        clip_copy[half, apart, index] = send(
            clip_piece(half, src_apart, index), clip_piece(half, apart, index),
            clip_send.at[half, apart, index], clip_recv.at[half, apart, index], along(half, step),
        )

    def text_step(distance, part):
        for step in (1, -1):
            dz = -distance % 8 if step == 1 else distance
            at = part if step == 1 else PARTS - 1 - part
            text_copy[dz, at].wait_recv()
            if distance < 3 or (distance == 3 and part < PARTS // 2):
                text_hop(dz, step, at)
            if distance == 4:
                if part == PARTS // 2 - 1:
                    core_part(4, 0 if step == 1 else 1)
            elif part == PARTS - 1:
                text_core(dz)

    def clip_pass(index):
        for half in (0, 1):
            clip_copy[half, 0, index].wait_recv()
            for step in (1, -1) if index < 2 else (-1, 1):
                clip_second(half, 0, index, step)

    def clip_on(index):
        for half in (0, 1):
            if index < 2:
                clip_copy[half, 3, index].wait_recv()
                clip_second(half, 3, index, 1)
            else:
                clip_copy[half, 1, index].wait_recv()
                clip_second(half, 1, index, -1)

    def clip_near():
        for half in (0, 1):
            for index in range(4):
                clip_copy[half, 1 if index < 2 else 3, index].wait_recv()

    def clip_far():
        for half in (0, 1):
            for index in range(4):
                clip_copy[half, 2, index].wait_recv()

    for part in range(PARTS):
        text_hop(0, 1, part)
        text_hop(0, -1, PARTS - 1 - part)
    for step in (1, -1, 2):
        for half in (0, 1):
            clip_first(half, step)
    for half in (0, 1):
        clip_second(half, 0, 0, 1)
        clip_second(half, 0, 0, -1)
    text_core(0)
    pos_copy = [
        send(posb.at[0], posb.at[(-step) % 4], pos_send.at[step], pos_recv.at[step], dev(dy=step)) for step in (1, 2, 3)
    ]

    lane = lax.broadcasted_iota(jnp.int32, (8, 128), 1)
    for dz in range(8):
        az = (z + dz) % 8
        base = (x * 4 + az // 2) * 1024 + (y * 4 + (az % 2) * 2) * ROWS
        ids = jnp.where(lane < ROWS, base + k * ROWS, base + (1 - k) * ROWS) + lane % ROWS
        colid[:, pl.ds(text_at(dz, 0), 128)] = ids.astype(F32)
    temp = jnp.exp(given_ref[0:1, 0:1])
    bias = given_ref[1:2, 0:1]
    factor = temp * LOG2E
    offset = bias * LOG2E
    acc[...] = jnp.zeros_like(acc)

    def fold(value):
        rows, columns = value.shape
        wide = jnp.sum(value.reshape(rows // 8, 8, columns), axis=0)
        return sum(wide[:, at:at + 128] for at in range(0, columns, 128))

    def piece(top, bottom, first, last):
        rows = pl.ds(top * 256, (bottom - top) * 256)
        columns = pl.ds(first * 128, (last - first) * 128)
        sims = lax.dot_general(clu[rows, :], txu[columns, :], (((1,), (1,)), ((), ())), preferred_element_type=F32)
        e = jnp.exp2(sims * factor + offset)
        plus = 1.0 + e
        inverse = 1.0 / plus
        mask = posc[rows, :] == colid[0:1, columns]
        dlogit = jnp.where(mask, -inverse, e * inverse)
        four = plus.reshape(4, plus.shape[0] // 4, plus.shape[1])
        acc[0] += fold(jnp.log((four[0] * four[1]) * (four[2] * four[3])))
        acc[1] += fold(dlogit)
        acc[2] += fold(dlogit * sims)
        acc[3] += fold(jnp.where(mask, sims, 0.0))
        dl[rows, columns] = dlogit.astype(BF16)

    def text_grad(first, last, top=0, bottom=4):
        rows = pl.ds(first * 128, (last - first) * 128)
        over = pl.ds(top * 256, (bottom - top) * 256)
        part = lax.dot_general(dl[over, rows], clu[over, :], (((0,), (0,)), ((), ())), preferred_element_type=F32)
        gt[rows, :] = part if top == 0 else gt[rows, :] + part

    def clip_grad(block, first=0, last=8):
        rows = pl.ds(block * 256, 256)
        over = pl.ds(first * 128, (last - first) * 128)
        part = lax.dot_general(dl[rows, over], txu[over, :], (((1,), (0,)), ((), ())), preferred_element_type=F32)
        gc[rows, :] = part if first == 0 else gc[rows, :] + part

    def positives():
        for copy in pos_copy:
            copy.wait_recv()
        z_hi = z // 2
        row_in = lax.broadcasted_iota(jnp.int32, (HALF, 128), 0)
        lane_in = lax.broadcasted_iota(jnp.int32, (HALF, 128), 1)
        for half in (0, 1):
            hit = lane_in == row_in + ((z_hi % 2) * ROWS + half * HALF)
            for dx in range(4):
                for dy in range(4):
                    apart, index = (dy, dx) if half == 0 else (dx, dy)
                    row = ((x + dx) % 4) * 2 + z_hi // 2
                    values = posb[dy, pl.ds(row, 1), :].astype(F32)
                    posc[pl.ds(clip_at(half, apart, index), HALF), :] = jnp.sum(
                        jnp.where(hit, values, 0.0), axis=1, keepdims=True
                    )

    def text_ready(*groups):
        for dz in groups:
            for copy in core_copy[dz]:
                copy.wait_recv()

    text_step(1, 0)
    clip_pass(1)
    clip_pass(3)
    text_step(1, 1)
    text_step(1, 2)
    clip_pass(2)
    text_step(1, 3)
    positives()
    text_step(2, 0)
    clip_on(0)
    clip_on(3)
    text_step(2, 1)
    text_step(2, 2)
    clip_on(1)
    clip_on(2)
    text_step(2, 3)
    text_ready(0, 1, 7, 2)
    piece(0, 1, 0, 4)
    text_step(3, 0)
    text_step(3, 1)
    clip_near()
    piece(1, 3, 0, 4)
    text_step(3, 2)
    text_step(3, 3)
    clip_grad(0, 0, 4)
    clip_grad(1, 0, 4)
    clip_grad(2, 0, 4)
    text_step(4, 0)
    text_step(4, 1)
    text_ready(6, 3, 5, 4)
    piece(0, 3, 4, 8)
    clip_far()
    piece(3, 4, 0, 8)

    def share(slots, targets):
        return [
            send(sums.at[slots[0]], sumr.at[slot], s_send.at[slot], s_recv.at[slot], to)
            for slot, to in zip(slots, targets)
        ]

    def collect(copies, slots, nxt):
        total = sums[slots[0]]
        for copy, slot in zip(copies, slots):
            copy.wait_recv()
            total = total + sumr[slot]
        sums[nxt] = total

    core_slots, x_slots, y_slots, z_slots = (0,), (1, 2, 3), (4, 5, 6), tuple(range(7, 14))

    def first_sums():
        for i in range(4):
            sums[0, pl.ds(i, 1), :] = jnp.sum(acc[i], axis=0, keepdims=True)
        sums[0, pl.ds(4, 4), :] = jnp.zeros((4, 128), F32)

    k_copy = {}

    def to_core(dz):
        ks[dz] = gt[pl.ds(text_at(dz, 1), ROWS), :].astype(BF16)
        k_copy[dz] = send(ks.at[dz], kr.at[dz], k_send.at[dz], k_recv.at[dz], dev(dk=1))

    def text_sum(dz, part):
        rows = pl.ds(part * CHUNK, CHUNK)
        return gt[pl.ds(text_at(dz, 0) + part * CHUNK, CHUNK), :] + kr[dz, rows, :].astype(F32)

    z_copy = {}

    def ring(stage, part):
        for way in (0, 1):
            dz = 4 - stage if way == 0 else 4 + stage
            at = part if way == 0 else PARTS - 1 - part
            rows = pl.ds(at * CHUNK, CHUNK)
            value = text_sum(dz, at)
            if stage > 1 or (stage == 1 and part < PARTS // 2):
                z_copy[way, stage - 1, at].wait_recv()
                value = value + zr[way, stage - 1, rows, :].astype(F32)
            zs[dz, rows, :] = value.astype(BF16)
            z_copy[way, stage, at] = send(
                zs.at[dz, rows], zr.at[way, stage, rows], z_send.at[way, stage, at], z_recv.at[way, stage, at],
                dev(dz=1 if way == 0 else -1),
            )

    def core_back(dz):
        k_copy[dz].wait_recv()

    c1_copy = {}
    c2_copy = {}
    c3_copy = {}

    def clip_r1(*indices):
        for index in indices:
            for half in (0, 1):
                cs1[half, index] = gc[pl.ds(clip_at(half, 2, index), HALF), :].astype(BF16)
                c1_copy[half, index] = send(
                    cs1.at[half, index], cr1.at[half, index], c1_send.at[half, index], c1_recv.at[half, index],
                    along(half, 1 if index < 2 else -1),
                )

    def clip_r2(way, *indices):
        apart = 1 if way == 0 else 3
        for index in indices:
            for half in (0, 1):
                value = gc[pl.ds(clip_at(half, apart, index), HALF), :]
                if (index < 2) == (way == 0):
                    c1_copy[half, index].wait_recv()
                    value = value + cr1[half, index].astype(F32)
                cs2[half, way, index] = value.astype(BF16)
                c2_copy[half, way, index] = send(
                    cs2.at[half, way, index], cr2.at[half, way, index],
                    c2_send.at[half, way, index], c2_recv.at[half, way, index],
                    along(half, 1 if way == 0 else -1),
                )

    def clip_r3(index):
        for half in (0, 1):
            value = gc[pl.ds(clip_at(half, 0, index), HALF), :]
            for way in (0, 1):
                c2_copy[half, way, index].wait_recv()
                value = value + cr2[half, way, index].astype(F32)
            if index == 0:
                gc[pl.ds(clip_at(half, 0, 0), HALF), :] = value
            else:
                cs3[half, index - 1] = value.astype(BF16)
                c3_copy[half, index] = send(
                    cs3.at[half, index - 1], cr3.at[half, index - 1],
                    c3_send.at[half, index - 1], c3_recv.at[half, index - 1], across(half, index),
                )

    text_grad(6, 8)
    to_core(4)
    to_core(5)
    clip_grad(3)
    clip_r1(1, 2)
    clip_r1(0, 3)
    core_back(4)
    ring(0, 0)
    ring(0, 1)
    first_sums()
    core_share = share(core_slots, [dev(dk=1)])
    text_grad(4, 6)
    to_core(3)
    to_core(6)
    clip_grad(1, 4)
    clip_r2(0, 2, 3)
    clip_grad(2, 4)
    clip_r2(1, 1, 0)
    core_back(3)
    core_back(5)
    ring(1, 2)
    ring(1, 3)
    collect(core_share, core_slots, 1)
    x_share = share(x_slots, [dev(dx=i) for i in (1, 2, 3)])
    text_grad(2, 4)
    to_core(2)
    to_core(7)
    ring(1, 0)
    clip_r2(0, 1)
    clip_r2(1, 2)
    ring(1, 1)
    clip_r2(0, 0)
    clip_r2(1, 3)
    collect(x_share, x_slots, 4)
    y_share = share(y_slots, [dev(dy=i) for i in (1, 2, 3)])
    clip_grad(0, 4)
    core_back(2)
    core_back(6)
    ring(2, 2)
    ring(2, 3)
    text_grad(0, 2)
    to_core(1)
    to_core(0)
    ring(2, 0)
    clip_r3(2)
    clip_r3(1)
    ring(2, 1)
    collect(y_share, y_slots, 7)
    z_share = share(z_slots, [dev(dz=i) for i in range(1, 8)])
    clip_r3(3)
    clip_r3(0)
    core_back(1)
    core_back(7)
    ring(3, 2)
    ring(3, 3)
    ring(3, 0)
    ring(3, 1)
    core_back(0)

    def finish(scale, normal, back):
        return scale * (back - normal * jnp.sum(normal * back, axis=1, keepdims=True))

    def finish_text(part):
        rows = pl.ds(part * CHUNK, CHUNK)
        value = text_sum(0, part)
        for way in (0, 1):
            z_copy[way, 3, part].wait_recv()
            value = value + zr[way, 3, rows, :].astype(F32)
        grad_text_ref[rows, :] = finish(text_scale[rows, :], text_norm[rows, :], value)

    def finish_clip(half):
        rows = pl.ds(half * HALF, HALF)
        value = gc[pl.ds(clip_at(half, 0, 0), HALF), :]
        for index in (1, 3, 2):
            c3_copy[half, index].wait_recv()
            value = value + cr3[half, index - 1].astype(F32)
        grad_clip_ref[rows, :] = finish(clip_scale[rows, :], clip_norm[rows, :], value)

    for half in (0, 1):
        finish_clip(half)
    for part in range(PARTS):
        finish_text(part)
    collect(z_share, z_slots, 14)

    total = jnp.sum(sums[14], axis=1, keepdims=True)
    pairs = 16384.0
    loss = (total[0:1] - temp * total[3:4]) / pairs - bias
    for i, value in enumerate((loss, temp * total[2:3] / pairs, total[1:2] / pairs)):
        scalar_ref[pl.ds(i, 1), :] = jnp.broadcast_to(value, (1, 128))

    for copy in started:
        copy.wait_send()


def per_device(clip_emb, text_emb, positive, log_temp, bias):
    vmem = pl.BlockSpec(memory_space=pltpu.VMEM)
    rows = jax.ShapeDtypeStruct((ROWS, D), F32)
    dma = pltpu.SemaphoreType.DMA
    given = jnp.where(lax.broadcasted_iota(jnp.int32, (8, 128), 0) == 0, log_temp, bias)
    grad_clip, grad_text, scalars = pl.pallas_call(
        kernel,
        out_shape=(rows, rows, jax.ShapeDtypeStruct((8, 128), F32)),
        in_specs=[vmem] * 3,
        out_specs=(vmem, vmem, vmem),
        scratch_shapes=[
            pltpu.VMEM((ROWS, D), F32),
            pltpu.VMEM((ROWS, 1), F32),
            pltpu.VMEM((ROWS, D), F32),
            pltpu.VMEM((ROWS, 1), F32),
            pltpu.VMEM((TILE, D), BF16),
            pltpu.VMEM((TILE, D), BF16),
            pltpu.VMEM((4, 8, 128), jnp.int32),
            pltpu.VMEM((TILE, 1), F32),
            pltpu.VMEM((8, TILE), F32),
            pltpu.VMEM((TILE, TILE), BF16),
            pltpu.VMEM((TILE, D), F32),
            pltpu.VMEM((TILE, D), F32),
            pltpu.VMEM((4, 8, 128), F32),
            pltpu.VMEM((2, 4, HALF, D), BF16),
            pltpu.VMEM((2, 4, HALF, D), BF16),
            pltpu.VMEM((2, 2, 4, HALF, D), BF16),
            pltpu.VMEM((2, 2, 4, HALF, D), BF16),
            pltpu.VMEM((2, 3, HALF, D), BF16),
            pltpu.VMEM((2, 3, HALF, D), BF16),
            pltpu.VMEM((8, ROWS, D), BF16),
            pltpu.VMEM((8, ROWS, D), BF16),
            pltpu.VMEM((8, ROWS, D), BF16),
            pltpu.VMEM((2, 4, ROWS, D), BF16),
            pltpu.VMEM((15, 8, 128), F32),
            pltpu.VMEM((14, 8, 128), F32),
            dma((2, 4, 4)), dma((2, 4, 4)), dma((8, PARTS)), dma((8, PARTS)), dma((9,)), dma((9,)), dma((4,)), dma((4,)),
            dma((2, 4)), dma((2, 4)), dma((2, 2, 4)), dma((2, 2, 4)), dma((2, 3)), dma((2, 3)),
            dma((8,)), dma((8,)), dma((2, 4, PARTS)), dma((2, 4, PARTS)), dma((14,)), dma((14,)),
        ],
        compiler_params=pltpu.CompilerParams(
            collective_id=0, has_side_effects=True, vmem_limit_bytes=50 * 2**20
        ),
        cost_estimate=pl.CostEstimate(flops=7247757312, bytes_accessed=900000, transcendentals=3 * 2**20),
    )(jnp.concatenate([clip_emb, text_emb[0]]), positive.reshape(8, 128), given)
    temp = jnp.exp(log_temp)
    grad_clip, grad_text = lax.optimization_barrier((temp * grad_clip, temp * grad_text))
    return scalars[0, 0], grad_clip, grad_text[None], scalars[1, 0], scalars[2, 0]


def solution(mesh):
    return jax.shard_map(
        per_device,
        mesh=mesh,
        in_specs=(P(("clip", "text"), None), P("text", "clip", None), P("clip"), P(), P()),
        out_specs=(P(), P(("clip", "text"), None), P("text", "clip", None), P(), P()),
        check_vma=False,
    )
```

```python
import jax
import jax.numpy as jnp
from jax import lax
from jax.experimental import pallas as pl
from jax.experimental.pallas import tpu as pltpu
from jax.sharding import PartitionSpec as P

MESH = pl.DeviceIdType.MESH
F32 = jnp.float32
BF16 = jnp.bfloat16
LOG2E = 1.4426950408889634
D = 1152
ROWS = 64
HALF = 32
TILE = 1024

CLIP_BLOCK = {0: 0, 1: 1, 3: 2, 2: 3}
TEXT_GROUP = {0: 0, 1: 1, 7: 2, 2: 3, 6: 4, 3: 5, 5: 6, 4: 7}
CHUNK = 16
PARTS = ROWS // CHUNK


def clip_at(half, apart, index):
    return CLIP_BLOCK[apart] * 256 + half * 128 + index * HALF


def text_at(dz, dk):
    return TEXT_GROUP[dz] * 128 + dk * ROWS


def kernel(
    emb_ref, pos_ref, log_temp_ref, bias_ref,
    grad_clip_ref, grad_text_ref, scalar_ref,
    clip_norm, clip_scale, text_norm, text_scale,
    clu, txu, posb, posc, colid, dl, gc, gt, acc,
    cs1, cr1, cs2, cr2, cs3, cr3, ks, kr, zs, zr, sums, sumr,
    clip_send, clip_recv, text_send, text_recv, core_send, core_recv, pos_send, pos_recv,
    c1_send, c1_recv, c2_send, c2_recv, c3_send, c3_recv, k_send, k_recv, z_send, z_recv, s_send, s_recv,
):
    c = lax.axis_index("clip")
    t = lax.axis_index("text")
    x, y, z, k = t // 4, c // 4, (t % 4) * 2 + (c // 2) % 2, c % 2

    def dev(dx=0, dy=0, dz=0, dk=0):
        ax, ay, az, ak = (x + dx) % 4, (y + dy) % 4, (z + dz) % 8, (k + dk) % 2
        return (ay * 4 + (az % 2) * 2 + ak, ax * 4 + az // 2)

    def along(half, step):
        return dev(dy=step) if half == 0 else dev(dx=step)

    def across(half, step):
        return dev(dx=step) if half == 0 else dev(dy=step)

    started = []

    def send(src, dst, ssem, rsem, to):
        copy = pltpu.make_async_remote_copy(
            src_ref=src, dst_ref=dst, send_sem=ssem, recv_sem=rsem, device_id=to, device_id_type=MESH
        )
        copy.start()
        started.append(copy)
        return copy

    peers = [dev(dx=i) for i in (1, 2, 3)] + [dev(dy=i) for i in (1, 2, 3)]
    peers += [dev(dz=i) for i in (1, 7)] + [dev(dk=1)]
    barrier = pltpu.get_barrier_semaphore()
    for peer in peers:
        pl.semaphore_signal(barrier, inc=1, device_id=peer, device_id_type=MESH)
    def unit_rows(first, scale_ref, norm_ref):
        wide = emb_ref[pl.ds(first, ROWS), :].astype(F32)
        scale = lax.rsqrt(jnp.sum(wide * wide, axis=1, keepdims=True) + 1e-06)
        normal = wide * scale
        scale_ref[...] = scale
        norm_ref[...] = normal
        return normal.astype(BF16)

    clip_unit = unit_rows(0, clip_scale, clip_norm)
    for half in (0, 1):
        clu[pl.ds(clip_at(half, 0, 0), HALF), :] = clip_unit[half * HALF:(half + 1) * HALF, :]
    txu[pl.ds(text_at(0, 0), ROWS), :] = unit_rows(ROWS, text_scale, text_norm)
    posb[0] = pos_ref[...]

    pl.semaphore_wait(barrier, len(peers))

    def text_piece(dz, dk, part):
        return txu.at[pl.ds(text_at(dz, dk) + part * CHUNK, CHUNK)]

    text_copy = {}

    def text_hop(src_dz, step, part):
        dst_dz = (src_dz - step) % 8
        text_copy[dst_dz, part] = send(
            text_piece(src_dz, 0, part), text_piece(dst_dz, 0, part),
            text_send.at[dst_dz, part], text_recv.at[dst_dz, part], dev(dz=step),
        )

    core_copy = {}

    def text_core(dz):
        rows = pl.ds(text_at(dz, 0), ROWS)
        core_copy[dz] = [
            send(txu.at[rows], txu.at[pl.ds(text_at(dz, 1), ROWS)], core_send.at[dz], core_recv.at[dz], dev(dk=1))
        ]

    def core_part(dz, half):
        mine, other = [pl.ds(text_at(dz, dk) + half * HALF, HALF) for dk in (0, 1)]
        copy = send(txu.at[mine], txu.at[other], core_send.at[dz + half * 4], core_recv.at[dz + half * 4], dev(dk=1))
        core_copy.setdefault(dz, []).append(copy)

    clip_copy = {}

    def clip_piece(half, apart, index):
        return clu.at[pl.ds(clip_at(half, apart, index), HALF)]

    def clip_first(half, step):
        index = (-step) % 4
        clip_copy[half, 0, index] = send(
            clip_piece(half, 0, 0), clip_piece(half, 0, index),
            clip_send.at[half, 0, index], clip_recv.at[half, 0, index], across(half, step),
        )

    def clip_second(half, src_apart, index, step):
        apart = (src_apart - step) % 4
        clip_copy[half, apart, index] = send(
            clip_piece(half, src_apart, index), clip_piece(half, apart, index),
            clip_send.at[half, apart, index], clip_recv.at[half, apart, index], along(half, step),
        )

    def text_step(distance, part):
        for step in (1, -1):
            dz = -distance % 8 if step == 1 else distance
            at = part if step == 1 else PARTS - 1 - part
            text_copy[dz, at].wait_recv()
            if distance < 3 or (distance == 3 and part < PARTS // 2):
                text_hop(dz, step, at)
            if distance == 4:
                if part == PARTS // 2 - 1:
                    core_part(4, 0 if step == 1 else 1)
            elif part == PARTS - 1:
                text_core(dz)

    def clip_pass(index):
        for half in (0, 1):
            clip_copy[half, 0, index].wait_recv()
            for step in (1, -1) if index < 2 else (-1, 1):
                clip_second(half, 0, index, step)

    def clip_on(index):
        for half in (0, 1):
            if index < 2:
                clip_copy[half, 3, index].wait_recv()
                clip_second(half, 3, index, 1)
            else:
                clip_copy[half, 1, index].wait_recv()
                clip_second(half, 1, index, -1)

    def clip_near():
        for half in (0, 1):
            for index in range(4):
                clip_copy[half, 1 if index < 2 else 3, index].wait_recv()

    def clip_far():
        for half in (0, 1):
            for index in range(4):
                clip_copy[half, 2, index].wait_recv()

    for step in (1, -1, 2):
        for half in (0, 1):
            clip_first(half, step)
    for part in range(PARTS):
        text_hop(0, 1, part)
        text_hop(0, -1, PARTS - 1 - part)
    for half in (0, 1):
        clip_second(half, 0, 0, 1)
        clip_second(half, 0, 0, -1)
    text_core(0)
    pos_copy = [
        send(posb.at[0], posb.at[(-step) % 4], pos_send.at[step], pos_recv.at[step], dev(dy=step)) for step in (1, 2, 3)
    ]

    lane = lax.broadcasted_iota(jnp.int32, (8, 128), 1)
    for dz in range(8):
        az = (z + dz) % 8
        base = (x * 4 + az // 2) * 1024 + (y * 4 + (az % 2) * 2) * ROWS
        ids = jnp.where(lane < ROWS, base + k * ROWS, base + (1 - k) * ROWS) + lane % ROWS
        colid[:, pl.ds(text_at(dz, 0), 128)] = ids.astype(F32)
    temp = jnp.exp(log_temp_ref[...])
    bias = bias_ref[...]
    factor = temp * LOG2E
    offset = bias * LOG2E
    acc[...] = jnp.zeros_like(acc)

    def fold(value):
        rows, columns = value.shape
        wide = jnp.sum(value.reshape(rows // 8, 8, columns), axis=0)
        return sum(wide[:, at:at + 128] for at in range(0, columns, 128))

    def piece(top, bottom, first, last):
        rows = pl.ds(top * 256, (bottom - top) * 256)
        columns = pl.ds(first * 128, (last - first) * 128)
        sims = lax.dot_general(clu[rows, :], txu[columns, :], (((1,), (1,)), ((), ())), preferred_element_type=F32)
        e = jnp.exp2(sims * factor + offset)
        plus = 1.0 + e
        inverse = 1.0 / plus
        mask = posc[rows, :] == colid[0:1, columns]
        dlogit = jnp.where(mask, -inverse, e * inverse)
        four = plus.reshape(4, plus.shape[0] // 4, plus.shape[1])
        acc[0] += fold(jnp.log((four[0] * four[1]) * (four[2] * four[3])))
        acc[1] += fold(dlogit)
        acc[2] += fold(dlogit * sims)
        acc[3] += fold(jnp.where(mask, sims, 0.0))
        dl[rows, columns] = dlogit.astype(BF16)

    def text_grad(first, last, top=0, bottom=4):
        rows = pl.ds(first * 128, (last - first) * 128)
        over = pl.ds(top * 256, (bottom - top) * 256)
        part = lax.dot_general(dl[over, rows], clu[over, :], (((0,), (0,)), ((), ())), preferred_element_type=F32)
        gt[rows, :] = part if top == 0 else gt[rows, :] + part

    def clip_grad(block, first=0, last=8):
        rows = pl.ds(block * 256, 256)
        over = pl.ds(first * 128, (last - first) * 128)
        part = lax.dot_general(dl[rows, over], txu[over, :], (((1,), (0,)), ((), ())), preferred_element_type=F32)
        gc[rows, :] = part if first == 0 else gc[rows, :] + part

    def positives():
        for copy in pos_copy:
            copy.wait_recv()
        z_hi = z // 2
        row_in = lax.broadcasted_iota(jnp.int32, (HALF, 128), 0)
        lane_in = lax.broadcasted_iota(jnp.int32, (HALF, 128), 1)
        for half in (0, 1):
            hit = lane_in == row_in + ((z_hi % 2) * ROWS + half * HALF)
            for dx in range(4):
                for dy in range(4):
                    apart, index = (dy, dx) if half == 0 else (dx, dy)
                    row = ((x + dx) % 4) * 2 + z_hi // 2
                    values = posb[dy, pl.ds(row, 1), :].astype(F32)
                    posc[pl.ds(clip_at(half, apart, index), HALF), :] = jnp.sum(
                        jnp.where(hit, values, 0.0), axis=1, keepdims=True
                    )

    def text_ready(*groups):
        for dz in groups:
            for copy in core_copy[dz]:
                copy.wait_recv()

    text_step(1, 0)
    clip_pass(1)
    clip_pass(3)
    text_step(1, 1)
    text_step(1, 2)
    clip_pass(2)
    text_step(1, 3)
    text_step(2, 0)
    clip_on(0)
    clip_on(3)
    text_step(2, 1)
    text_step(2, 2)
    clip_on(1)
    clip_on(2)
    text_step(2, 3)
    positives()
    text_ready(0, 1, 7, 2)
    piece(0, 1, 0, 4)
    text_step(3, 0)
    text_step(3, 1)
    clip_near()
    piece(1, 3, 0, 4)
    text_step(3, 2)
    text_step(3, 3)
    clip_grad(0, 0, 4)
    clip_grad(1, 0, 4)
    clip_grad(2, 0, 4)
    text_ready(6, 3, 5)
    piece(0, 3, 4, 7)
    text_step(4, 0)
    text_step(4, 1)
    clip_far()
    piece(3, 4, 0, 7)
    text_ready(4)
    piece(0, 4, 7, 8)

    def share(slots, targets):
        return [
            send(sums.at[slots[0]], sumr.at[slot], s_send.at[slot], s_recv.at[slot], to)
            for slot, to in zip(slots, targets)
        ]

    def collect(copies, slots, nxt):
        total = sums[slots[0]]
        for copy, slot in zip(copies, slots):
            copy.wait_recv()
            total = total + sumr[slot]
        sums[nxt] = total

    core_slots, x_slots, y_slots, z_slots = (0,), (1, 2, 3), (4, 5, 6), tuple(range(7, 14))

    def first_sums():
        for i in range(4):
            sums[0, pl.ds(i, 1), :] = jnp.sum(acc[i], axis=0, keepdims=True)
        sums[0, pl.ds(4, 4), :] = jnp.zeros((4, 128), F32)

    k_copy = {}

    def to_core(dz):
        ks[dz] = gt[pl.ds(text_at(dz, 1), ROWS), :].astype(BF16)
        k_copy[dz] = send(ks.at[dz], kr.at[dz], k_send.at[dz], k_recv.at[dz], dev(dk=1))

    def text_sum(dz, part):
        rows = pl.ds(part * CHUNK, CHUNK)
        return gt[pl.ds(text_at(dz, 0) + part * CHUNK, CHUNK), :] + kr[dz, rows, :].astype(F32)

    z_copy = {}

    def ring(stage, part):
        for way in (0, 1):
            dz = 4 - stage if way == 0 else 4 + stage
            at = part if way == 0 else PARTS - 1 - part
            rows = pl.ds(at * CHUNK, CHUNK)
            value = text_sum(dz, at)
            if stage > 1 or (stage == 1 and part < PARTS // 2):
                z_copy[way, stage - 1, at].wait_recv()
                value = value + zr[way, stage - 1, rows, :].astype(F32)
            zs[dz, rows, :] = value.astype(BF16)
            z_copy[way, stage, at] = send(
                zs.at[dz, rows], zr.at[way, stage, rows], z_send.at[way, stage, at], z_recv.at[way, stage, at],
                dev(dz=1 if way == 0 else -1),
            )

    def core_back(dz):
        k_copy[dz].wait_recv()

    c1_copy = {}
    c2_copy = {}
    c3_copy = {}

    def clip_r1(*indices):
        for index in indices:
            for half in (0, 1):
                cs1[half, index] = gc[pl.ds(clip_at(half, 2, index), HALF), :].astype(BF16)
                c1_copy[half, index] = send(
                    cs1.at[half, index], cr1.at[half, index], c1_send.at[half, index], c1_recv.at[half, index],
                    along(half, 1 if index < 2 else -1),
                )

    def clip_r2(way, *indices):
        apart = 1 if way == 0 else 3
        for index in indices:
            for half in (0, 1):
                value = gc[pl.ds(clip_at(half, apart, index), HALF), :]
                if (index < 2) == (way == 0):
                    c1_copy[half, index].wait_recv()
                    value = value + cr1[half, index].astype(F32)
                cs2[half, way, index] = value.astype(BF16)
                c2_copy[half, way, index] = send(
                    cs2.at[half, way, index], cr2.at[half, way, index],
                    c2_send.at[half, way, index], c2_recv.at[half, way, index],
                    along(half, 1 if way == 0 else -1),
                )

    def clip_r3(index):
        for half in (0, 1):
            value = gc[pl.ds(clip_at(half, 0, index), HALF), :]
            for way in (0, 1):
                c2_copy[half, way, index].wait_recv()
                value = value + cr2[half, way, index].astype(F32)
            if index == 0:
                gc[pl.ds(clip_at(half, 0, 0), HALF), :] = value
            else:
                cs3[half, index - 1] = value.astype(BF16)
                c3_copy[half, index] = send(
                    cs3.at[half, index - 1], cr3.at[half, index - 1],
                    c3_send.at[half, index - 1], c3_recv.at[half, index - 1], across(half, index),
                )

    text_grad(7, 8)
    to_core(4)
    clip_grad(3)
    clip_r1(1, 2)
    clip_r1(0, 3)
    core_back(4)
    ring(0, 0)
    ring(0, 1)
    first_sums()
    core_share = share(core_slots, [dev(dk=1)])
    text_grad(5, 7)
    to_core(3)
    to_core(5)
    clip_grad(1, 4)
    clip_r2(0, 2, 3)
    clip_grad(2, 4)
    clip_r2(1, 1, 0)
    core_back(3)
    core_back(5)
    ring(1, 2)
    ring(1, 3)
    collect(core_share, core_slots, 1)
    x_share = share(x_slots, [dev(dx=i) for i in (1, 2, 3)])
    text_grad(3, 5)
    to_core(2)
    to_core(6)
    ring(1, 0)
    clip_r2(0, 1)
    clip_r2(1, 2)
    ring(1, 1)
    clip_r2(0, 0)
    clip_r2(1, 3)
    collect(x_share, x_slots, 4)
    y_share = share(y_slots, [dev(dy=i) for i in (1, 2, 3)])
    clip_grad(0, 4)
    core_back(2)
    core_back(6)
    ring(2, 2)
    ring(2, 3)
    text_grad(0, 3)
    to_core(1)
    to_core(7)
    to_core(0)
    ring(2, 0)
    ring(2, 1)
    core_back(1)
    core_back(7)
    ring(3, 2)
    collect(y_share, y_slots, 7)
    z_share = share(z_slots, [dev(dz=i) for i in range(1, 8)])
    clip_r3(2)
    clip_r3(1)
    ring(3, 3)
    ring(3, 0)
    clip_r3(3)
    clip_r3(0)
    ring(3, 1)
    core_back(0)

    half_temp = 0.5 * temp

    def finish(scale, normal, back):
        return scale * (back - normal * jnp.sum(normal * back, axis=1, keepdims=True))

    def finish_text(part):
        rows = pl.ds(part * CHUNK, CHUNK)
        value = text_sum(0, part)
        for way in (0, 1):
            z_copy[way, 3, part].wait_recv()
            value = value + zr[way, 3, rows, :].astype(F32)
        grad_text_ref[rows, :] = finish(half_temp * text_scale[rows, :], text_norm[rows, :], value)

    def finish_clip(half):
        rows = pl.ds(half * HALF, HALF)
        value = gc[pl.ds(clip_at(half, 0, 0), HALF), :]
        for index in (1, 3, 2):
            c3_copy[half, index].wait_recv()
            value = value + cr3[half, index - 1].astype(F32)
        grad_clip_ref[rows, :] = finish(half_temp * clip_scale[rows, :], clip_norm[rows, :], value)

    for half in (0, 1):
        finish_clip(half)
    for part in range(PARTS):
        finish_text(part)
    collect(z_share, z_slots, 14)

    total = jnp.sum(sums[14], axis=1, keepdims=True)
    pairs = 16384.0
    loss = (total[0:1] - temp * total[3:4]) / pairs - bias
    for i, value in enumerate((loss, temp * total[2:3] / pairs, total[1:2] / pairs)):
        scalar_ref[pl.ds(i, 1), :] = jnp.broadcast_to(value, (1, 128))

    for copy in started:
        copy.wait_send()


def per_device(clip_emb, text_emb, positive, log_temp, bias):
    vmem = pl.BlockSpec(memory_space=pltpu.VMEM)
    rows = jax.ShapeDtypeStruct((ROWS, D), F32)
    dma = pltpu.SemaphoreType.DMA
    grad_clip, grad_text, scalars = pl.pallas_call(
        kernel,
        out_shape=(rows, rows, jax.ShapeDtypeStruct((8, 128), F32)),
        in_specs=[vmem] * 4,
        out_specs=(vmem, vmem, vmem),
        scratch_shapes=[
            pltpu.VMEM((ROWS, D), F32),
            pltpu.VMEM((ROWS, 1), F32),
            pltpu.VMEM((ROWS, D), F32),
            pltpu.VMEM((ROWS, 1), F32),
            pltpu.VMEM((TILE, D), BF16),
            pltpu.VMEM((TILE, D), BF16),
            pltpu.VMEM((4, 8, 128), jnp.int32),
            pltpu.VMEM((TILE, 1), F32),
            pltpu.VMEM((8, TILE), F32),
            pltpu.VMEM((TILE, TILE), BF16),
            pltpu.VMEM((TILE, D), F32),
            pltpu.VMEM((TILE, D), F32),
            pltpu.VMEM((4, 8, 128), F32),
            pltpu.VMEM((2, 4, HALF, D), BF16),
            pltpu.VMEM((2, 4, HALF, D), BF16),
            pltpu.VMEM((2, 2, 4, HALF, D), BF16),
            pltpu.VMEM((2, 2, 4, HALF, D), BF16),
            pltpu.VMEM((2, 3, HALF, D), BF16),
            pltpu.VMEM((2, 3, HALF, D), BF16),
            pltpu.VMEM((8, ROWS, D), BF16),
            pltpu.VMEM((8, ROWS, D), BF16),
            pltpu.VMEM((8, ROWS, D), BF16),
            pltpu.VMEM((2, 4, ROWS, D), BF16),
            pltpu.VMEM((15, 8, 128), F32),
            pltpu.VMEM((14, 8, 128), F32),
            dma((2, 4, 4)), dma((2, 4, 4)), dma((8, PARTS)), dma((8, PARTS)), dma((9,)), dma((9,)), dma((4,)), dma((4,)),
            dma((2, 4)), dma((2, 4)), dma((2, 2, 4)), dma((2, 2, 4)), dma((2, 3)), dma((2, 3)),
            dma((8,)), dma((8,)), dma((2, 4, PARTS)), dma((2, 4, PARTS)), dma((14,)), dma((14,)),
        ],
        compiler_params=pltpu.CompilerParams(
            collective_id=0, has_side_effects=True, vmem_limit_bytes=50 * 2**20
        ),
        cost_estimate=pl.CostEstimate(flops=7247757312, bytes_accessed=900000, transcendentals=3 * 2**20),
    )(jnp.concatenate([clip_emb, text_emb[0]]), positive.reshape(8, 128), log_temp.reshape(1, 1), bias.reshape(1, 1))
    grad_clip, grad_text = lax.optimization_barrier((2.0 * grad_clip, 2.0 * grad_text))
    return scalars[0, 0], grad_clip, grad_text[None], scalars[1, 0], scalars[2, 0]


def solution(mesh):
    return jax.shard_map(
        per_device,
        mesh=mesh,
        in_specs=(P(("clip", "text"), None), P("text", "clip", None), P("clip"), P(), P()),
        out_specs=(P(), P(("clip", "text"), None), P("text", "clip", None), P(), P()),
        check_vma=False,
    )
```
